32 devices in a mesh: blk: 16 (over z, y, core), rep: 2 (over x).
Axes of the slice: x: 2, y: 2, z: 4, core: 2. Of those that a mesh axis runs over, the one named last changes fastest.
Arguments:
- features: bfloat16 [8192, 512], P(('blk', 'rep')), may hold values from -6 to 6
- tile_values: bfloat16 [16, 2, 96, 128, 128], P('blk', 'rep'), may hold values from -0.078125 to 0.078125
- tile_rows: int32 [16, 2, 96], P('blk', 'rep'), may hold values from 0 to 3, as said below
- tile_cols: int32 [16, 2, 96], P('blk', 'rep'), may hold values from 0 to 31, as said below
- tile_counts: int32 [16, 2], P('blk', 'rep'), may hold values from 21 to 96, as said below
- weight: bfloat16 [512, 512], replicated, may hold values from -0.25 to 0.25
- bias: float32 [512], replicated, may hold values from -3 to 3
- head: float32 [2, 512], replicated, may hold values from -0.125 to 0.125
- times: float32 [8192], P(('blk', 'rep')), may hold values from 0.3 to 3
- events: int32 [8192], P(('blk', 'rep')), may hold values 0 or 1
Outputs:
- hidden: bfloat16 [8192, 512], P(('blk', 'rep'))
- grad_weight: float32 [512, 512], replicated
- grad_bias: float32 [512], replicated
- grad_head: float32 [2, 512], replicated
The draws below stay inside these ranges and needn't reach their ends.
Inputs may be any that keep to these rules, and one draw needn't show every extreme that they name: `tile_rows`: row tile of a slot within the row block of its device. `tile_cols`: within the live slots of one device no (row, column) pair repeats; each source block c is read by at most 6 live slots of one device, and by exactly 6 for some source block of every device. `tile_counts`: live slots come first, grouped by source block in increasing order of block; every source block has at least one live slot on every device; slots past the count hold arbitrary indices.
All inputs are finite; a program needn't handle non-finite values. No bound on the sum of `events` on one device may be relied on, other than what follows from the above.
Results may differ from the reference program's by a relative error of at most 0.0044.
Values may be sent and summed in bfloat16 or wider, within the bound.
A program may use at most 64 MiB of HBM per device.

```python
import math
import jax
import jax.numpy as jnp
from jax import lax

F = 512
TILE = 128
MOST = 6
R_DEV = 256
SLOTS = 96
NODES = 8192
N_BLK = 16
N_REP = 2


def tile_layout(key):
    row_tiles = R_DEV * N_REP // TILE
    col_tiles = R_DEV // TILE
    places = row_tiles * col_tiles
    slots = MOST * N_BLK
    devices = N_BLK * N_REP
    key_level, key_full, key_count, key_order, key_pad_row, key_pad_col = jax.random.split(key, 6)
    level = jax.random.randint(key_level, (devices, 1), MOST // 2, MOST + 1)
    per_source = jax.random.randint(key_count, (devices, N_BLK), 0, 1 << 20) % level + 1
    device_index = jnp.arange(devices)[:, None]
    per_source = jnp.where(device_index == 0, MOST, per_source)
    per_source = jnp.where(device_index == devices - 1, 1, per_source)
    full_source = jax.random.randint(key_full, (devices, 1), 0, N_BLK)
    per_source = jnp.where(jnp.arange(N_BLK)[None, :] == full_source, MOST, per_source)
    order_keys = jax.random.randint(key_order, (devices, N_BLK, places), 0, 1 << 16) * places + jnp.arange(places)[None, None, :]
    order = jnp.argsort(order_keys, axis=-1)[:, :, :MOST]
    offsets = jnp.cumsum(per_source, axis=1) - per_source
    within = jnp.arange(MOST)[None, None, :]
    target = jnp.where(within < per_source[:, :, None], offsets[:, :, None] + within, slots)
    live_rows = order // col_tiles
    live_cols = jnp.arange(N_BLK)[None, :, None] * col_tiles + order % col_tiles
    pad_rows = jax.random.randint(key_pad_row, (devices, slots), 0, row_tiles)
    pad_cols = jax.random.randint(key_pad_col, (devices, slots), 0, N_BLK * col_tiles)
    device_ids = jnp.broadcast_to(jnp.arange(devices)[:, None, None], target.shape)
    row_ids = pad_rows.at[device_ids, target].set(live_rows, mode='drop')
    col_ids = pad_cols.at[device_ids, target].set(live_cols, mode='drop')
    counts = jnp.sum(per_source, axis=1)
    return (row_ids.reshape(N_BLK, N_REP, slots).astype(jnp.int32), col_ids.reshape(N_BLK, N_REP, slots).astype(jnp.int32), counts.reshape(N_BLK, N_REP).astype(jnp.int32))


def draw_tile_rows(key, part):
    return tile_layout(jax.random.fold_in(key, 7))[0]


def draw_tile_cols(key, part):
    return tile_layout(jax.random.fold_in(key, 7))[1]


def draw_tile_counts(key, part):
    return tile_layout(jax.random.fold_in(key, 7))[2]


def with_ends(drawn, rng, low, top_value):
    dims = drawn.shape
    place = [jax.random.randint(jax.random.fold_in(rng, axis), (), 0, dims[axis]) for axis in range(len(dims))]
    drawn = drawn.at[tuple(place)].set(low)
    longest = dims.index(max(dims))
    place[longest] = (place[longest] + 1) % dims[longest]
    return drawn.at[tuple(place)].set(top_value)


def block_scale(own_key, dims, pieces, low, top_value):
    factor_of = 1.0
    for axis_at, blocks in pieces:
        steps = jax.random.uniform(jax.random.fold_in(jax.random.fold_in(own_key, 6), axis_at), (blocks,), jnp.float32, low / len(pieces), top_value / len(pieces))
        factor_of = factor_of * jnp.repeat(jnp.exp(steps), dims[axis_at] // blocks).reshape((-1,) + (1,) * (len(dims) - 1 - axis_at))
    return factor_of


def normal_values(rng, shape, width, most, pieces=(), held_as=jnp.bfloat16):
    values = jax.random.normal(rng, shape, jnp.float32) * width
    if len(pieces) > 0:
        values = block_scale(rng, shape, pieces, -0.22, 0.18) * values
    return jnp.clip(values, min=-most, max=most).astype(held_as)


def setup_inputs(seed: int = 0) -> dict:
    seeds = jax.random.split(jax.random.key(seed), 11)
    features = normal_values(seeds[0], (NODES, F), 1.0, 6.0, ((0, 32),))
    tile_values = normal_values(seeds[1], (N_BLK, N_REP, SLOTS, TILE, TILE), (MOST * N_BLK * TILE * TILE // R_DEV) ** -0.5, 0.078125, ((0, 16), (1, 2)))
    tile_rows = draw_tile_rows(jax.random.fold_in(seeds[10], 71), 0)
    tile_cols = draw_tile_cols(jax.random.fold_in(seeds[10], 71), 0)
    tile_counts = draw_tile_counts(jax.random.fold_in(seeds[10], 71), 0)
    weight = normal_values(seeds[5], (F, F), F ** -0.5, 0.25)
    bias = normal_values(seeds[6], (F,), 0.5, 3.0, (), jnp.float32)
    head = normal_values(seeds[7], (2, F), (4 * F) ** -0.5, 0.125, (), jnp.float32)
    times = jnp.clip(jnp.exp(math.log(3.0) - 2.3025851 * jax.random.uniform(seeds[8], (NODES,), jnp.float32) ** block_scale(seeds[8], (NODES,), ((0, 32),), -0.2, 0.2)), 0.3, 3.0)
    events = with_ends((jax.random.randint(seeds[9], (NODES,), 0, 2) < 1).astype(jnp.int32), jax.random.fold_in(seeds[9], 1), 0, 1)
    return {"features": features, "tile_values": tile_values, "tile_rows": tile_rows, "tile_cols": tile_cols, "tile_counts": tile_counts, "weight": weight, "bias": bias, "head": head, "times": times, "events": events}


def reference(features, tile_values, tile_rows, tile_cols, tile_counts, weight, bias, head, times, events):
    row_tiles = R_DEV * N_REP // TILE
    col_tiles = R_DEV // TILE
    slots = MOST * N_BLK
    sources = features.reshape(N_BLK, N_REP, col_tiles, TILE, F)

    def owner_rows(owner):
        total = jnp.zeros((row_tiles, TILE, F), jnp.float32)
        for replica in range(N_REP):
            col_ids = tile_cols[owner, replica]
            picked = sources[col_ids // col_tiles, replica, col_ids % col_tiles]
            in_use = jnp.arange(slots) < tile_counts[owner, replica]
            products = jnp.einsum('kij,kjf->kif', tile_values[owner, replica].astype(jnp.float32), picked.astype(jnp.float32))
            placing = ((tile_rows[owner, replica][:, None] == jnp.arange(row_tiles)[None, :]) & in_use[:, None]).astype(jnp.float32)
            total = total + jnp.einsum('kr,kif->rif', placing, products, precision=lax.Precision.HIGHEST)
        return total
    aggregated = lax.map(owner_rows, jnp.arange(N_BLK)).reshape(NODES, F)
    aggregated_bf = aggregated.astype(jnp.bfloat16)
    preact = jnp.dot(aggregated_bf, weight, preferred_element_type=jnp.float32) + bias
    hidden = jax.nn.silu(preact).astype(jnp.bfloat16)
    hidden_wide = lax.optimization_barrier(hidden).astype(jnp.float32)
    scores = jnp.dot(hidden_wide, head.T, precision=lax.Precision.HIGHEST)
    scale_log = scores[:, 0]
    shape_param = jax.nn.softplus(scores[:, 1]) + 0.5
    log_ratio = jnp.log(times) - scale_log
    hazard = jnp.exp(shape_param * log_ratio)
    observed = events.astype(jnp.float32)
    norm_factor = 1.0 / math.sqrt(NODES)
    grad_scale = (observed * shape_param - shape_param * hazard) * norm_factor
    grad_shape = (hazard * log_ratio - observed * (1.0 / shape_param + log_ratio)) * jax.nn.sigmoid(scores[:, 1]) * norm_factor
    stacked = jnp.stack([grad_scale, grad_shape], axis=1)
    grad_head = jnp.dot(stacked.T, hidden_wide, precision=lax.Precision.HIGHEST)
    sigmoid_pre = jax.nn.sigmoid(preact)
    grad_hidden = grad_scale[:, None] * head[0][None, :] + grad_shape[:, None] * head[1][None, :]
    grad_preact = grad_hidden * sigmoid_pre * (1.0 + preact * (1.0 - sigmoid_pre))
    grad_bias = lax.optimization_barrier(jnp.sum(grad_preact, axis=0))
    grad_preact_bf = grad_preact.astype(jnp.bfloat16)
    grad_weight = jnp.dot(aggregated_bf.T, grad_preact_bf, preferred_element_type=jnp.float32)
    return (hidden, grad_weight, grad_bias, grad_head)
```

```python
import functools
import math

import jax
import jax.numpy as jnp
from jax import lax
from jax.experimental import pallas as pl
from jax.experimental.pallas import tpu as pltpu
from jax.sharding import PartitionSpec as P

MOST = 6
MESH = pl.DeviceIdType.MESH
F32 = jnp.float32
BF16 = jnp.bfloat16


def fused_sum_rows(owners, replicas, width):
    group = 2 * replicas
    line = owners // 4
    half = width // 2
    if owners % 4 or half % (group * line) or (half // (group * line)) % 16:
        return None
    return half, half // group, half // (group * line)


def kernel(
    owners, replicas, pieces,
    feats, tiles_hbm, rows_ref, cols_ref, count_ref, weight_hbm, bias_ref, head_ref, times_ref, events_ref,
    hidden_ref, gw_ref, small_ref,
    gath, dense, tiles, weight, acc, xsend, xrecv, agg, pre, slope,
    gsum, g1s, g1r, g2s, g2r, g3s, g3r, sm_send, sm1, sm2, sm3,
    local_sem, ring_send, ring_recv, mate_send, mate_recv, x_send, x_recv, g_send, g_recv, s_send, s_recv,
):
    chips = owners // 2
    far = chips // 2
    slots = tiles_hbm.shape[0]
    tile = tiles_hbm.shape[1]
    here = feats.shape[0]
    width = feats.shape[1]
    half = width // 2
    col_tiles = here // tile
    row_tiles = here * replicas // tile
    unit = here // 2

    b = lax.axis_index("blk")
    r = lax.axis_index("rep")
    core = lax.rem(b, 2)
    chip = lax.div(b, 2)
    y = lax.rem(chip, 2)
    z = lax.div(chip, 2)
    pos = (1 - y) * z + y * (chips - 1 - z)
    mate = chip * 2 + 1 - core

    def block_at(position):
        upper = lax.div(position, far)
        depth = (1 - upper) * position + upper * (chips - 1 - position)
        return (2 * depth + upper) * 2 + core

    def from_me(d, h):
        return block_at(lax.rem(pos + (chips - h if d == 0 else h), chips))

    def mate_of(block):
        return block + 1 - 2 * core

    right, left = from_me(1, 1), from_me(0, 1)

    def reach(d, u):
        return far if d == u else far - 1

    def ring(d, s, u, h, block):
        ref = gath.at[s, block, pl.ds(u * unit, unit)]
        return pltpu.make_async_remote_copy(
            src_ref=ref, dst_ref=ref,
            send_sem=ring_send.at[d, s, u, h], recv_sem=ring_recv.at[d, s, u, h],
            device_id=(right if d == 0 else left, r), device_id_type=MESH,
        )

    def to_mate(d, s, u, h, block):
        ref = gath.at[s, block, pl.ds(u * unit, unit)]
        return pltpu.make_async_remote_copy(
            src_ref=ref, dst_ref=ref,
            send_sem=mate_send.at[d, s, u, h], recv_sem=mate_recv.at[d, s, u, h],
            device_id=(mate, r), device_id_type=MESH,
        )

    own = [pltpu.make_async_copy(feats.at[:, pl.ds(s * half, half)], gath.at[s, b], local_sem.at[s]) for s in range(2)]
    own[0].start()
    own[1].start()
    get_tiles = pltpu.make_async_copy(tiles_hbm, tiles.at[pl.ds(0, slots)], local_sem.at[2])
    get_tiles.start()
    get_weight = pltpu.make_async_copy(weight_hbm, weight, local_sem.at[3])
    get_weight.start()

    group = 2 * replicas
    line = owners // 4
    in_group = y * replicas + r

    def group_peer(o):
        other = lax.rem(in_group + o, group)
        return ((z * 2 + lax.div(other, replicas)) * 2 + core, lax.rem(other, replicas))

    def line_peer(o):
        return ((lax.rem(z + o, line) * 2 + y) * 2 + core, r)

    greeted = [(right, r), (left, r), (mate, r)]
    greeted += [(b, lax.rem(r + o, replicas)) for o in range(1, replicas)]
    if pieces:
        greeted += [group_peer(o) for o in range(1, group)] + [line_peer(o) for o in range(1, line)]
    barrier = pltpu.get_barrier_semaphore()
    for peer in greeted:
        pl.semaphore_signal(barrier, inc=1, device_id=peer, device_id_type=MESH)
    pl.semaphore_wait(barrier, len(greeted))

    sent = []

    def start(copy):
        copy.start()
        sent.append(copy)

    def send_own(s):
        for u in range(2):
            for d in range(2):
                start(ring(d, s, u, 0, b))
        for u in range(2):
            start(to_mate(0, s, u, 0, b))

    def arrive(s, h):
        for u in range(2):
            for d in range(2):
                if h > reach(d, u):
                    continue
                block = from_me(d, h)
                ring(d, s, u, h - 1, block).wait_recv()
                if h + 1 <= reach(d, u):
                    start(ring(d, s, u, h, block))
                start(to_mate(d, s, u, h, block))

    def arrive_mate(s, h):
        for u in range(2):
            for d in range(2):
                if h == 0:
                    if d == 0:
                        to_mate(0, s, u, 0, mate).wait_recv()
                elif h <= reach(d, u):
                    to_mate(d, s, u, h, mate_of(from_me(d, h))).wait_recv()

    tiles[slots] = jnp.zeros((tile, tile), BF16)
    count = count_ref[0, 0]

    def fill(source, first):
        picked = [jnp.int32(slots)] * (row_tiles * col_tiles)
        run = jnp.int32(0)
        for k in range(MOST):
            slot = first + k
            safe = jnp.minimum(slot, slots - 1)
            q = cols_ref[0, 0, safe]
            ok = (slot < count) & (q >= source * col_tiles) & (q < (source + 1) * col_tiles)
            key = jnp.where(ok, rows_ref[0, 0, safe] * col_tiles + q - source * col_tiles, -1)
            run = run + ok.astype(jnp.int32)
            picked = [jnp.where(key == at, slot, old) for at, old in enumerate(picked)]
        for at, slot in enumerate(picked):
            i, j = at // col_tiles, at % col_tiles
            dense[source, i * tile:(i + 1) * tile, j * tile:(j + 1) * tile] = tiles[slot]
        return first + run

    def product(s, part, block):
        a = dense[block, pl.ds(pl.multiple_of(part * here, here), here), :]
        return jnp.dot(a, gath[s, block], preferred_element_type=F32)

    def multiply(s, part, blocks):
        total = acc[s, part]
        for block in blocks:
            total = total + product(s, part, block)
        acc[s, part] = total

    def blocks_at(h):
        if h == 0:
            return [b, mate]
        ones = [from_me(0, h)] if h == far else [from_me(0, h), from_me(1, h)]
        return ones + [mate_of(block) for block in ones]

    def to_rep(s, o):
        return pltpu.make_async_remote_copy(
            src_ref=xsend.at[s, o - 1], dst_ref=xrecv.at[s, o - 1],
            send_sem=x_send.at[s, o - 1], recv_sem=x_recv.at[s, o - 1],
            device_id=(b, lax.rem(r + o, replicas)), device_id_type=MESH,
        )

    def settle(s):
        total = acc[s, r]
        for o in range(1, replicas):
            to_rep(s, o).wait_recv()
            total = total + xrecv[s, o - 1].astype(F32)
        agg[s] = total.astype(BF16)

    own[0].wait()
    own[1].wait()
    send_own(0)
    get_tiles.wait()
    first = jnp.int32(0)
    share = owners // far
    for h in range(1, far + 1):
        first = lax.fori_loop((h - 1) * share, h * share, fill, first)
        arrive(0, h)
        if h == far - 1:
            send_own(1)
    for h in range(far + 1):
        arrive_mate(0, h)
    arrive(1, 1)

    def first_half(part):
        def step(block, total):
            return total + product(0, part, block)
        return lax.fori_loop(0, owners, step, jnp.zeros((here, half), F32))

    for o in range(1, replicas):
        xsend[0, o - 1] = first_half(lax.rem(r + o, replicas)).astype(BF16)
        start(to_rep(0, o))
    acc[0, r] = first_half(r)

    arrive(1, 2)
    acc[1] = jnp.zeros((replicas, here, half), F32)
    for h in range(2):
        arrive_mate(1, h)
        for part in range(replicas):
            multiply(1, part, blocks_at(h))
    settle(0)
    get_weight.wait()
    pre[...] = jnp.dot(agg[0], weight[0:half, :], preferred_element_type=F32) + bias_ref[...]
    for h in range(3, far + 1):
        arrive(1, h)
        arrive_mate(1, h - 1)
        for part in range(replicas):
            multiply(1, part, blocks_at(h - 1))
    arrive_mate(1, far)
    for o in range(1, replicas):
        part = lax.rem(r + o, replicas)
        multiply(1, part, blocks_at(far))
        xsend[1, o - 1] = acc[1, part].astype(BF16)
        start(to_rep(1, o))
    multiply(1, r, blocks_at(far))
    settle(1)

    rows = 64
    for at in range(0, here, rows):
        p = pre[at:at + rows, :] + jnp.dot(agg[1, at:at + rows, :], weight[half:, :], preferred_element_type=F32)
        sig = 1.0 / (1.0 + jnp.exp(-p))
        hidden_ref[at:at + rows, :] = (p * sig).astype(BF16)
        slope[at:at + rows, :] = sig * (1.0 + p * (1.0 - sig))
    wide = hidden_ref[...].astype(F32)
    scores = lax.dot_general(
        head_ref[...], wide, (((1,), (1,)), ((), ())), precision=lax.Precision.HIGHEST, preferred_element_type=F32
    )
    scale_log = scores[0:1, :]
    raw = scores[1:2, :]
    shape_param = jnp.maximum(raw, 0.0) + jnp.log1p(jnp.exp(-jnp.abs(raw))) + 0.5
    log_ratio = jnp.log(times_ref[...]) - scale_log
    hazard = jnp.exp(shape_param * log_ratio)
    observed = events_ref[...].astype(F32)
    norm = 1.0 / math.sqrt(here * owners * replicas)
    grad_scale = (observed * shape_param - shape_param * hazard) * norm
    grad_shape = (
        (hazard * log_ratio - observed * (1.0 / shape_param + log_ratio)) * (1.0 / (1.0 + jnp.exp(-raw))) * norm
    )
    stacked = jnp.concatenate([grad_scale, grad_shape, jnp.zeros((6, here), F32)], axis=0)
    sm_send[0, 1:3, :] = jnp.dot(stacked, wide, precision=lax.Precision.HIGHEST, preferred_element_type=F32)[0:2]
    upright = stacked.T
    bias_sum = jnp.zeros((1, width), F32)
    for at in range(0, here, rows):
        gh = upright[at:at + rows, 0:1] * head_ref[0:1, :] + upright[at:at + rows, 1:2] * head_ref[1:2, :]
        gp = gh * slope[at:at + rows, :]
        bias_sum = bias_sum + jnp.sum(gp, axis=0, keepdims=True)
        pre[at:at + rows, :] = gp
    sm_send[0, 0:1, :] = bias_sum
    sm_send[0, 3:8, :] = jnp.zeros((5, width), F32)
    gp_bf = pre[...].astype(BF16)

    def grad_half(s):
        return lax.dot_general(agg[s], gp_bf, (((0,), (0,)), ((), ())), preferred_element_type=F32)

    if not pieces:
        gw_ref[0:half, :] = grad_half(0)
        gw_ref[half:, :] = grad_half(1)
        small_ref[...] = sm_send[0]
    else:
        big, mid, low = pieces

        def remote(src, dst, sems, at, peer):
            return pltpu.make_async_remote_copy(
                src_ref=src, dst_ref=dst, send_sem=sems[0].at[at], recv_sem=sems[1].at[at],
                device_id=peer, device_id_type=MESH,
            )

        gs, ss = (g_send, g_recv), (s_send, s_recv)
        partner = (mate, r)
        c_small = remote(sm_send.at[0], sm1, ss, 0, partner)
        start(c_small)
        g1s[...] = grad_half(1 - core).astype(BF16)
        c_big = remote(g1s, g1r, gs, 0, partner)
        start(c_big)
        mine = grad_half(core)
        c_small.wait_recv()
        sm_send[1] = sm_send[0] + sm1[...]
        small2 = [remote(sm_send.at[1], sm2.at[o - 1], ss, o, group_peer(o)) for o in range(1, group)]
        for copy in small2:
            start(copy)
        c_big.wait_recv()
        gsum[...] = mine + g1r[...].astype(F32)
        copies = []
        for o in range(1, group):
            other = lax.rem(in_group + o, group)
            g2s[o - 1] = gsum[pl.ds(pl.multiple_of(other * mid, mid), mid), :].astype(BF16)
            copy = remote(g2s.at[o - 1], g2r.at[o - 1], gs, o, group_peer(o))
            start(copy)
            copies.append(copy)
        for copy in small2:
            copy.wait_recv()
        total = sm_send[1]
        for o in range(1, group):
            total = total + sm2[o - 1]
        sm_send[2] = total
        small3 = [remote(sm_send.at[2], sm3.at[o - 1], ss, group - 1 + o, line_peer(o)) for o in range(1, line)]
        for copy in small3:
            start(copy)
        first_row = pl.multiple_of(in_group * mid, mid)
        for copy in copies:
            copy.wait_recv()
        total = gsum[pl.ds(first_row, mid), :]
        for o in range(1, group):
            total = total + g2r[o - 1].astype(F32)
        gsum[pl.ds(first_row, mid), :] = total
        copies = []
        for o in range(1, line):
            other = lax.rem(z + o, line)
            g3s[o - 1] = gsum[pl.ds(pl.multiple_of(first_row + other * low, low), low), :].astype(BF16)
            copy = remote(g3s.at[o - 1], g3r.at[o - 1], gs, group - 1 + o, line_peer(o))
            start(copy)
            copies.append(copy)
        for copy in small3:
            copy.wait_recv()
        total = sm_send[2]
        for o in range(1, line):
            total = total + sm3[o - 1]
        small_ref[...] = total
        for copy in copies:
            copy.wait_recv()
        total = gsum[pl.ds(pl.multiple_of(first_row + z * low, low), low), :]
        for o in range(1, line):
            total = total + g3r[o - 1].astype(F32)
        base = core * big
        spot = pl.multiple_of(base + first_row + z * low, low)
        gw_ref[pl.ds(spot, low), :] = total.astype(BF16)
        used = group + line - 1
        for o in range(1, line):
            ref = gw_ref.at[pl.ds(spot, low)]
            start(remote(ref, ref, gs, used + o - 1, line_peer(o)))
        for o in range(1, line):
            other = lax.rem(z + line - o, line)
            ref = gw_ref.at[pl.ds(pl.multiple_of(base + first_row + other * low, low), low)]
            remote(ref, ref, gs, used + o - 1, line_peer(o)).wait_recv()
        used = used + line - 1
        for o in range(1, group):
            ref = gw_ref.at[pl.ds(pl.multiple_of(base + first_row, mid), mid)]
            start(remote(ref, ref, gs, used + o - 1, group_peer(o)))
        for o in range(1, group):
            other = lax.rem(in_group + group - o, group)
            ref = gw_ref.at[pl.ds(pl.multiple_of(base + other * mid, mid), mid)]
            remote(ref, ref, gs, used + o - 1, group_peer(o)).wait_recv()
        used = used + group - 1
        ref = gw_ref.at[pl.ds(pl.multiple_of(base, big), big)]
        start(remote(ref, ref, gs, used, partner))
        ref = gw_ref.at[pl.ds(pl.multiple_of((1 - core) * big, big), big)]
        remote(ref, ref, gs, used, partner).wait_recv()
    for copy in sent:
        copy.wait_send()


def local(owners, replicas, features, tile_values, tile_rows, tile_cols, tile_counts, weight, bias, head, times, events):
    here, width = features.shape
    half = width // 2
    slots, tile = tile_values.shape[2], tile_values.shape[3]
    pieces = fused_sum_rows(owners, replicas, width)
    far = owners // 4
    group, line = 2 * replicas, max(owners // 4, 2)
    big, mid, low = pieces or (16, 16, 16)
    vmem = pl.BlockSpec(memory_space=pltpu.VMEM)
    smem = pl.BlockSpec(memory_space=pltpu.SMEM)
    hbm = pl.BlockSpec(memory_space=pl.ANY)
    dma = pltpu.SemaphoreType.DMA
    g_count = 2 * (group + line)
    hidden, grad_weight, small = pl.pallas_call(
        functools.partial(kernel, owners, replicas, pieces),
        out_shape=(
            jax.ShapeDtypeStruct((here, width), BF16),
            jax.ShapeDtypeStruct((width, width), BF16 if pieces else F32),
            jax.ShapeDtypeStruct((8, width), F32),
        ),
        in_specs=[hbm, hbm, smem, smem, smem, hbm, vmem, vmem, vmem, vmem],
        out_specs=(vmem, vmem, vmem),
        scratch_shapes=[
            pltpu.VMEM((2, owners, here, half), BF16),
            pltpu.VMEM((owners, here * replicas, here), BF16),
            pltpu.VMEM((slots + 1, tile, tile), BF16),
            pltpu.VMEM((width, width), BF16),
            pltpu.VMEM((2, replicas, here, half), F32),
            pltpu.VMEM((2, replicas - 1, here, half), BF16),
            pltpu.VMEM((2, replicas - 1, here, half), BF16),
            pltpu.VMEM((2, here, half), BF16),
            pltpu.VMEM((here, width), F32),
            pltpu.VMEM((here, width), F32),
            pltpu.VMEM((big, width), F32),
            pltpu.VMEM((big, width), BF16),
            pltpu.VMEM((big, width), BF16),
            pltpu.VMEM((group - 1, mid, width), BF16),
            pltpu.VMEM((group - 1, mid, width), BF16),
            pltpu.VMEM((line - 1, low, width), BF16),
            pltpu.VMEM((line - 1, low, width), BF16),
            pltpu.VMEM((3, 8, width), F32),
            pltpu.VMEM((8, width), F32),
            pltpu.VMEM((group - 1, 8, width), F32),
            pltpu.VMEM((line - 1, 8, width), F32),
            dma((4,)),
            dma((2, 2, 2, far)),
            dma((2, 2, 2, far)),
            dma((2, 2, 2, far + 1)),
            dma((2, 2, 2, far + 1)),
            dma((2, replicas - 1)),
            dma((2, replicas - 1)),
            dma((g_count,)),
            dma((g_count,)),
            dma((group + line,)),
            dma((group + line,)),
        ],
        compiler_params=pltpu.CompilerParams(
            collective_id=0, has_side_effects=True, vmem_limit_bytes=60 * 1024 * 1024
        ),
    )(
        features,
        tile_values.reshape(slots, tile, tile),
        tile_rows,
        tile_cols,
        tile_counts,
        weight,
        bias.reshape(1, width),
        head,
        times.reshape(1, here),
        events.reshape(1, here),
    )
    if pieces:
        grad_weight = grad_weight.astype(F32)
    else:
        grad_weight, small = lax.psum((grad_weight, small), ("blk", "rep"))
    return hidden, grad_weight, small[0], small[1:3]


def solution(mesh):
    placed = (
        P(("blk", "rep"), None),
        P("blk", "rep", None, None, None),
        P("blk", "rep", None),
        P("blk", "rep", None),
        P("blk", "rep"),
        P(),
        P(),
        P(),
        P(("blk", "rep")),
        P(("blk", "rep")),
    )
    return jax.shard_map(
        functools.partial(local, mesh.shape["blk"], mesh.shape["rep"]),
        mesh=mesh,
        in_specs=placed,
        out_specs=(P(("blk", "rep"), None), P(), P(), P()),
        check_vma=False,
    )
```

```python
import functools
import math

import jax
import jax.numpy as jnp
from jax import lax
from jax.experimental import pallas as pl
from jax.experimental.pallas import tpu as pltpu
from jax.sharding import PartitionSpec as P

MOST = 6
MESH = pl.DeviceIdType.MESH
F32 = jnp.float32
BF16 = jnp.bfloat16


def fused_sum_rows(owners, replicas, width):
    group = 2 * replicas
    line = owners // 4
    half = width // 2
    if owners % 4 or half % (group * line) or (half // (group * line)) % 16:
        return None
    return half, half // group, half // (group * line)


def kernel(
    owners, replicas, pieces,
    feats, tiles_hbm, rows_ref, cols_ref, count_ref, weight_hbm, bias_ref, head_ref, times_ref, events_ref,
    hidden_ref, gw_ref, small_ref,
    gath, dense, tiles, weight, acc, xsend0, xrecv0, xsend1, xrecv1, agg, pre, slope,
    gsum, g1s, g1r, g2s, g2r, g3s, g3r, sm_send, sm1, sm2, sm3,
    local_sem, ring_send, ring_recv, mate_send, mate_recv, x_send, x_recv, g_send, g_recv, s_send, s_recv,
):
    chips = owners // 2
    far = chips // 2
    slots = tiles_hbm.shape[0]
    tile = tiles_hbm.shape[1]
    here = feats.shape[0]
    width = feats.shape[1]
    half = width // 2
    col_tiles = here // tile
    row_tiles = here * replicas // tile
    unit = here // 2

    b = lax.axis_index("blk")
    r = lax.axis_index("rep")
    core = lax.rem(b, 2)
    chip = lax.div(b, 2)
    y = lax.rem(chip, 2)
    z = lax.div(chip, 2)
    pos = (1 - y) * z + y * (chips - 1 - z)
    mate = chip * 2 + 1 - core

    def block_at(position):
        upper = lax.div(position, far)
        depth = (1 - upper) * position + upper * (chips - 1 - position)
        return (2 * depth + upper) * 2 + core

    def from_me(d, h):
        return block_at(lax.rem(pos + (chips - h if d == 0 else h), chips))

    def mate_of(block):
        return block + 1 - 2 * core

    right, left = from_me(1, 1), from_me(0, 1)

    def reach(d, u):
        return far if d == u else far - 1

    def ring(d, s, u, h, block):
        ref = gath.at[s, block, pl.ds(u * unit, unit)]
        return pltpu.make_async_remote_copy(
            src_ref=ref, dst_ref=ref,
            send_sem=ring_send.at[d, s, u, h], recv_sem=ring_recv.at[d, s, u, h],
            device_id=(right if d == 0 else left, r), device_id_type=MESH,
        )

    def to_mate(d, s, u, h, block):
        ref = gath.at[s, block, pl.ds(u * unit, unit)]
        return pltpu.make_async_remote_copy(
            src_ref=ref, dst_ref=ref,
            send_sem=mate_send.at[d, s, u, h], recv_sem=mate_recv.at[d, s, u, h],
            device_id=(mate, r), device_id_type=MESH,
        )

    own = [pltpu.make_async_copy(feats.at[:, pl.ds(s * half, half)], gath.at[s, b], local_sem.at[s]) for s in range(2)]
    own[0].start()
    own[1].start()
    get_tiles = pltpu.make_async_copy(tiles_hbm, tiles.at[pl.ds(0, slots)], local_sem.at[2])
    get_tiles.start()
    get_weight = pltpu.make_async_copy(weight_hbm, weight, local_sem.at[3])
    get_weight.start()

    group = 2 * replicas
    line = owners // 4
    in_group = y * replicas + r

    def group_peer(o):
        other = lax.rem(in_group + o, group)
        return ((z * 2 + lax.div(other, replicas)) * 2 + core, lax.rem(other, replicas))

    def line_peer(o):
        return ((lax.rem(z + o, line) * 2 + y) * 2 + core, r)

    greeted = [(right, r), (left, r), (mate, r)]
    greeted += [(b, lax.rem(r + o, replicas)) for o in range(1, replicas)]
    if pieces:
        greeted += [group_peer(o) for o in range(1, group)] + [line_peer(o) for o in range(1, line)]
    barrier = pltpu.get_barrier_semaphore()
    for peer in greeted:
        pl.semaphore_signal(barrier, inc=1, device_id=peer, device_id_type=MESH)
    pl.semaphore_wait(barrier, len(greeted))

    sent = []

    def start(copy):
        copy.start()
        sent.append(copy)

    def send_own(s):
        for u in range(2):
            for d in range(2):
                start(ring(d, s, u, 0, b))
        for u in range(2):
            start(to_mate(0, s, u, 0, b))

    def arrive(s, h):
        for u in range(2):
            for d in range(2):
                if h > reach(d, u):
                    continue
                block = from_me(d, h)
                ring(d, s, u, h - 1, block).wait_recv()
                if h + 1 <= reach(d, u):
                    start(ring(d, s, u, h, block))
                start(to_mate(d, s, u, h, block))

    def arrive_mate(s, h):
        for u in range(2):
            for d in range(2):
                if h == 0:
                    if d == 0:
                        to_mate(0, s, u, 0, mate).wait_recv()
                elif h <= reach(d, u):
                    to_mate(d, s, u, h, mate_of(from_me(d, h))).wait_recv()

    tiles[slots] = jnp.zeros((tile, tile), BF16)
    count = count_ref[0, 0]

    def fill(source, first):
        picked = [jnp.int32(slots)] * (row_tiles * col_tiles)
        run = jnp.int32(0)
        for k in range(MOST):
            slot = first + k
            safe = jnp.minimum(slot, slots - 1)
            q = cols_ref[0, 0, safe]
            ok = (slot < count) & (q >= source * col_tiles) & (q < (source + 1) * col_tiles)
            key = jnp.where(ok, rows_ref[0, 0, safe] * col_tiles + q - source * col_tiles, -1)
            run = run + ok.astype(jnp.int32)
            picked = [jnp.where(key == at, slot, old) for at, old in enumerate(picked)]
        for at, slot in enumerate(picked):
            i, j = at // col_tiles, at % col_tiles
            dense[source, i * tile:(i + 1) * tile, j * tile:(j + 1) * tile] = tiles[slot]
        return first + run

    def product(s, part, block):
        a = dense[block, pl.ds(pl.multiple_of(part * here, here), here), :]
        return jnp.dot(a, gath[s, block], preferred_element_type=F32)

    def multiply(s, part, blocks):
        total = acc[s, part]
        for block in blocks:
            total = total + product(s, part, block)
        acc[s, part] = total

    def blocks_at(h):
        if h == 0:
            return [b, mate]
        ones = [from_me(0, h)] if h == far else [from_me(0, h), from_me(1, h)]
        return ones + [mate_of(block) for block in ones]

    def to_rep(s, o):
        return pltpu.make_async_remote_copy(
            src_ref=(xsend0, xsend1)[s].at[o - 1], dst_ref=(xrecv0, xrecv1)[s].at[o - 1],
            send_sem=x_send.at[s, o - 1], recv_sem=x_recv.at[s, o - 1],
            device_id=(b, lax.rem(r + o, replicas)), device_id_type=MESH,
        )

    def settle(s):
        total = acc[s, r]
        for o in range(1, replicas):
            to_rep(s, o).wait_recv()
            total = total + (xrecv0, xrecv1)[s][o - 1].astype(F32)
        agg[s] = total.astype(BF16)

    own[0].wait()
    own[1].wait()
    send_own(0)
    get_tiles.wait()
    first = jnp.int32(0)
    share = owners // far
    acc[1] = jnp.zeros((replicas, here, half), F32)
    for h in range(1, far + 1):
        first = lax.fori_loop((h - 1) * share, h * share, fill, first)
        arrive(0, h)
        if h == 1:
            send_own(1)
        else:
            arrive(1, h - 1)
    for h in range(far + 1):
        arrive_mate(0, h)

    def first_half(part):
        def step(block, total):
            return total + product(0, part, block)
        return lax.fori_loop(0, owners, step, jnp.zeros((here, half), F32))

    for o in range(1, replicas):
        xsend0[o - 1] = first_half(lax.rem(r + o, replicas))
        start(to_rep(0, o))
    arrive(1, far)
    for h in range(far):
        arrive_mate(1, h)
        for part in range(replicas):
            multiply(1, part, blocks_at(h))
    arrive_mate(1, far)
    for o in range(1, replicas):
        part = lax.rem(r + o, replicas)
        multiply(1, part, blocks_at(far))
        xsend1[o - 1] = acc[1, part].astype(BF16)
        start(to_rep(1, o))
    acc[0, r] = first_half(r)
    multiply(1, r, blocks_at(far))
    settle(0)
    get_weight.wait()
    pre[...] = jnp.dot(agg[0], weight[0:half, :], preferred_element_type=F32) + bias_ref[...]
    settle(1)

    rows = 64
    for at in range(0, here, rows):
        p = pre[at:at + rows, :] + jnp.dot(agg[1, at:at + rows, :], weight[half:, :], preferred_element_type=F32)
        sig = 1.0 / (1.0 + jnp.exp(-p))
        hidden_ref[at:at + rows, :] = (p * sig).astype(BF16)
        slope[at:at + rows, :] = sig * (1.0 + p * (1.0 - sig))
    wide = hidden_ref[...].astype(F32)
    scores = lax.dot_general(
        head_ref[...], wide, (((1,), (1,)), ((), ())), precision=lax.Precision.HIGHEST, preferred_element_type=F32
    )
    scale_log = scores[0:1, :]
    raw = scores[1:2, :]
    shape_param = jnp.maximum(raw, 0.0) + jnp.log1p(jnp.exp(-jnp.abs(raw))) + 0.5
    log_ratio = jnp.log(times_ref[...]) - scale_log
    hazard = jnp.exp(shape_param * log_ratio)
    observed = events_ref[...].astype(F32)
    norm = 1.0 / math.sqrt(here * owners * replicas)
    grad_scale = (observed * shape_param - shape_param * hazard) * norm
    grad_shape = (
        (hazard * log_ratio - observed * (1.0 / shape_param + log_ratio)) * (1.0 / (1.0 + jnp.exp(-raw))) * norm
    )
    stacked = jnp.concatenate([grad_scale, grad_shape, jnp.zeros((6, here), F32)], axis=0)
    sm_send[0, 1:3, :] = jnp.dot(stacked, wide, precision=lax.Precision.HIGHEST, preferred_element_type=F32)[0:2]
    upright = stacked.T
    bias_sum = jnp.zeros((1, width), F32)
    for at in range(0, here, rows):
        gh = upright[at:at + rows, 0:1] * head_ref[0:1, :] + upright[at:at + rows, 1:2] * head_ref[1:2, :]
        gp = gh * slope[at:at + rows, :]
        bias_sum = bias_sum + jnp.sum(gp, axis=0, keepdims=True)
        pre[at:at + rows, :] = gp
    sm_send[0, 0:1, :] = bias_sum
    sm_send[0, 3:8, :] = jnp.zeros((5, width), F32)
    gp_bf = pre[...].astype(BF16)

    def grad_half(s):
        return lax.dot_general(agg[s], gp_bf, (((0,), (0,)), ((), ())), preferred_element_type=F32)

    if not pieces:
        gw_ref[0:half, :] = grad_half(0)
        gw_ref[half:, :] = grad_half(1)
        small_ref[...] = sm_send[0]
    else:
        big, mid, low = pieces

        def remote(src, dst, sems, at, peer):
            return pltpu.make_async_remote_copy(
                src_ref=src, dst_ref=dst, send_sem=sems[0].at[at], recv_sem=sems[1].at[at],
                device_id=peer, device_id_type=MESH,
            )

        gs, ss = (g_send, g_recv), (s_send, s_recv)
        partner = (mate, r)
        base = core * big

        def from_group(o):
            return lax.rem(in_group + group - o, group)

        def from_line(o):
            return lax.rem(z + line - o, line)

        def piece(start_row, member, count):
            return pl.ds(pl.multiple_of(start_row + member * count, count), count)

        c_small = remote(sm_send.at[0], sm1, ss, 0, partner)
        start(c_small)
        g1s[...] = grad_half(1 - core).astype(BF16)
        order = [lax.rem(in_group + o, group) for o in range(1, group)] + [in_group]
        copies1 = []
        for at, member in enumerate(order):
            rows_of = piece(0, member, mid)
            copies1.append(remote(g1s.at[rows_of], g1r.at[rows_of], gs, at, partner))
            start(copies1[-1])
        gsum[...] = grad_half(core)
        c_small.wait_recv()
        sm_send[1] = sm_send[0] + sm1[...]
        small2 = [remote(sm_send.at[1], sm2.at[o - 1], ss, o, group_peer(o)) for o in range(1, group)]
        for copy in small2:
            start(copy)
        used = group
        copies = []
        for o in range(1, group):
            rows_of = piece(0, order[o - 1], mid)
            copies1[o - 1].wait_recv()
            g2s[o - 1] = (gsum[rows_of, :] + g1r[rows_of, :].astype(F32)).astype(BF16)
            copies.append(remote(g2s.at[o - 1], g2r.at[o - 1], gs, used + o - 1, group_peer(o)))
            start(copies[-1])
        used += group - 1
        copies1[group - 1].wait_recv()
        first_row = in_group * mid
        rows_of = piece(0, in_group, mid)
        total = gsum[rows_of, :] + g1r[rows_of, :].astype(F32)
        for copy in small2:
            copy.wait_recv()
        small_total = sm_send[1]
        for o in range(1, group):
            small_total = small_total + sm2[o - 1]
        sm_send[2] = small_total
        small3 = [remote(sm_send.at[2], sm3.at[o - 1], ss, group - 1 + o, line_peer(o)) for o in range(1, line)]
        for copy in small3:
            start(copy)
        for o in range(1, group):
            copies[o - 1].wait_recv()
            total = total + g2r[o - 1].astype(F32)
        gsum[rows_of, :] = total
        copies = []
        for o in range(1, line):
            g3s[o - 1] = gsum[piece(first_row, lax.rem(z + o, line), low), :].astype(BF16)
            copies.append(remote(g3s.at[o - 1], g3r.at[o - 1], gs, used + o - 1, line_peer(o)))
            start(copies[-1])
        used += line - 1
        total = gsum[piece(first_row, z, low), :]
        for o in range(1, line):
            copies[o - 1].wait_recv()
            total = total + g3r[o - 1].astype(F32)
        gw_ref[piece(base + first_row, z, low), :] = total.astype(BF16)

        def along_line(o, member):
            ref = gw_ref.at[piece(base + first_row, member, low)]
            return remote(ref, ref, gs, used + o - 1, line_peer(o))

        def in_plane(o, lo, from_member):
            ref = gw_ref.at[piece(base + from_member * mid, from_line(lo), low)]
            return remote(ref, ref, gs, used + (line - 1) + (o - 1) * line + lo, group_peer(o))

        def over_chip(o, lo, half_base):
            ref = gw_ref.at[piece(half_base + from_group(o) * mid, from_line(lo), low)]
            return remote(ref, ref, gs, used + (line - 1) + (group - 1) * line + o * line + lo, partner)

        for o in range(1, line):
            start(along_line(o, z))
        for lo in range(line):
            if lo:
                along_line(lo, from_line(lo)).wait_recv()
            for o in range(1, group):
                start(in_plane(o, lo, in_group))
            start(over_chip(0, lo, base))
        for copy in small3:
            copy.wait_recv()
        small_total = sm_send[2]
        for o in range(1, line):
            small_total = small_total + sm3[o - 1]
        small_ref[...] = small_total
        for lo in range(line):
            for o in range(1, group):
                in_plane(o, lo, from_group(o)).wait_recv()
                start(over_chip(o, lo, base))
        for lo in range(line):
            for o in range(group):
                over_chip(o, lo, (1 - core) * big).wait_recv()
    for copy in sent:
        copy.wait_send()


def finish(hidden_in, gw_in, small_in, hidden_out, gw_out, bias_out, head_out):
    hidden_out[...] = hidden_in[...]
    gw_out[...] = gw_in[...].astype(F32)
    bias_out[...] = small_in[0, :]
    head_out[...] = small_in[1:3, :]


def local(owners, replicas, features, tile_values, tile_rows, tile_cols, tile_counts, weight, bias, head, times, events):
    here, width = features.shape
    half = width // 2
    slots, tile = tile_values.shape[2], tile_values.shape[3]
    pieces = fused_sum_rows(owners, replicas, width)
    far = owners // 4
    group, line = 2 * replicas, max(owners // 4, 2)
    big, mid, low = pieces or (16, 16, 16)
    vmem = pl.BlockSpec(memory_space=pltpu.VMEM)
    smem = pl.BlockSpec(memory_space=pltpu.SMEM)
    hbm = pl.BlockSpec(memory_space=pl.ANY)
    dma = pltpu.SemaphoreType.DMA
    g_count = 2 * group + 2 * line + 2 * group * line
    hidden, grad_weight, small = pl.pallas_call(
        functools.partial(kernel, owners, replicas, pieces),
        out_shape=(
            jax.ShapeDtypeStruct((here, width), BF16),
            jax.ShapeDtypeStruct((width, width), BF16 if pieces else F32),
            jax.ShapeDtypeStruct((8, width), F32),
        ),
        in_specs=[hbm, hbm, smem, smem, smem, hbm, vmem, vmem, vmem, vmem],
        out_specs=(vmem, vmem, vmem),
        scratch_shapes=[
            pltpu.VMEM((2, owners, here, half), BF16),
            pltpu.VMEM((owners, here * replicas, here), BF16),
            pltpu.VMEM((slots + 1, tile, tile), BF16),
            pltpu.VMEM((width, width), BF16),
            pltpu.VMEM((2, replicas, here, half), F32),
            pltpu.VMEM((replicas - 1, here, half), F32),
            pltpu.VMEM((replicas - 1, here, half), F32),
            pltpu.VMEM((replicas - 1, here, half), BF16),
            pltpu.VMEM((replicas - 1, here, half), BF16),
            pltpu.VMEM((2, here, half), BF16),
            pltpu.VMEM((here, width), F32),
            pltpu.VMEM((here, width), F32),
            pltpu.VMEM((big, width), F32),
            pltpu.VMEM((big, width), BF16),
            pltpu.VMEM((big, width), BF16),
            pltpu.VMEM((group - 1, mid, width), BF16),
            pltpu.VMEM((group - 1, mid, width), BF16),
            pltpu.VMEM((line - 1, low, width), BF16),
            pltpu.VMEM((line - 1, low, width), BF16),
            pltpu.VMEM((3, 8, width), F32),
            pltpu.VMEM((8, width), F32),
            pltpu.VMEM((group - 1, 8, width), F32),
            pltpu.VMEM((line - 1, 8, width), F32),
            dma((4,)),
            dma((2, 2, 2, far)),
            dma((2, 2, 2, far)),
            dma((2, 2, 2, far + 1)),
            dma((2, 2, 2, far + 1)),
            dma((2, replicas - 1)),
            dma((2, replicas - 1)),
            dma((g_count,)),
            dma((g_count,)),
            dma((group + line,)),
            dma((group + line,)),
        ],
        compiler_params=pltpu.CompilerParams(
            collective_id=0, has_side_effects=True, vmem_limit_bytes=60 * 1024 * 1024
        ),
    )(
        features,
        tile_values.reshape(slots, tile, tile),
        tile_rows,
        tile_cols,
        tile_counts,
        weight,
        bias.reshape(1, width),
        head,
        times.reshape(1, here),
        events.reshape(1, here),
    )
    if not pieces:
        grad_weight, small = lax.psum((grad_weight, small), ("blk", "rep"))
    return pl.pallas_call(
        finish,
        out_shape=(
            jax.ShapeDtypeStruct((here, width), BF16),
            jax.ShapeDtypeStruct((width, width), F32),
            jax.ShapeDtypeStruct((width,), F32),
            jax.ShapeDtypeStruct((2, width), F32),
        ),
        in_specs=[vmem, vmem, vmem],
        out_specs=(vmem, vmem, vmem, vmem),
    )(hidden, grad_weight, small)


def solution(mesh):
    placed = (
        P(("blk", "rep"), None),
        P("blk", "rep", None, None, None),
        P("blk", "rep", None),
        P("blk", "rep", None),
        P("blk", "rep"),
        P(),
        P(),
        P(),
        P(("blk", "rep")),
        P(("blk", "rep")),
    )
    return jax.shard_map(
        functools.partial(local, mesh.shape["blk"], mesh.shape["rep"]),
        mesh=mesh,
        in_specs=placed,
        out_specs=(P(("blk", "rep"), None), P(), P(), P()),
        check_vma=False,
    )
```

```python
import functools
import math

import jax
import jax.numpy as jnp
from jax import lax
from jax.experimental import pallas as pl
from jax.experimental.pallas import tpu as pltpu
from jax.sharding import PartitionSpec as P

MOST = 6
MESH = pl.DeviceIdType.MESH
F32 = jnp.float32
BF16 = jnp.bfloat16


def fused_sum_rows(owners, replicas, width):
    group = 2 * replicas
    line = owners // 4
    half = width // 2
    if owners % 4 or half % (group * line) or (half // (group * line)) % 16:
        return None
    return half, half // group, half // (group * line)


def kernel(
    owners, replicas, pieces,
    feats, tiles_hbm, rows_ref, cols_ref, count_ref, weight_hbm, bias_ref, head_ref, times_ref, events_ref,
    hidden_ref, gw_ref, small_ref,
    gath, dense, tiles, weight, acc, xsend0, xrecv0, xsend1, xrecv1, agg, pre, slope,
    gsum, g1s, g1r, g2s, g2r, g3s, g3r, sm_send, sm1, sm2, sm3,
    local_sem, ring_send, ring_recv, mate_send, mate_recv, x_send, x_recv, g_send, g_recv, s_send, s_recv,
):
    chips = owners // 2
    far = chips // 2
    slots = tiles_hbm.shape[0]
    tile = tiles_hbm.shape[1]
    here = feats.shape[0]
    width = feats.shape[1]
    half = width // 2
    col_tiles = here // tile
    row_tiles = here * replicas // tile
    unit = here // 2

    b = lax.axis_index("blk")
    r = lax.axis_index("rep")
    core = lax.rem(b, 2)
    chip = lax.div(b, 2)
    y = lax.rem(chip, 2)
    z = lax.div(chip, 2)
    pos = (1 - y) * z + y * (chips - 1 - z)
    mate = chip * 2 + 1 - core

    def block_at(position):
        upper = lax.div(position, far)
        depth = (1 - upper) * position + upper * (chips - 1 - position)
        return (2 * depth + upper) * 2 + core

    def from_me(d, h):
        return block_at(lax.rem(pos + (chips - h if d == 0 else h), chips))

    def mate_of(block):
        return block + 1 - 2 * core

    right, left = from_me(1, 1), from_me(0, 1)

    def reach(d, u):
        return far if d == u else far - 1

    def ring(d, s, u, h, block):
        ref = gath.at[s, block, pl.ds(u * unit, unit)]
        return pltpu.make_async_remote_copy(
            src_ref=ref, dst_ref=ref,
            send_sem=ring_send.at[d, s, u, h], recv_sem=ring_recv.at[d, s, u, h],
            device_id=(right if d == 0 else left, r), device_id_type=MESH,
        )

    def to_mate(d, s, u, h, block):
        ref = gath.at[s, block, pl.ds(u * unit, unit)]
        return pltpu.make_async_remote_copy(
            src_ref=ref, dst_ref=ref,
            send_sem=mate_send.at[d, s, u, h], recv_sem=mate_recv.at[d, s, u, h],
            device_id=(mate, r), device_id_type=MESH,
        )

    own = [pltpu.make_async_copy(feats.at[:, pl.ds(s * half, half)], gath.at[s, b], local_sem.at[s]) for s in range(2)]
    own[0].start()
    own[1].start()
    get_tiles = pltpu.make_async_copy(tiles_hbm, tiles.at[pl.ds(0, slots)], local_sem.at[2])
    get_tiles.start()
    get_weight = pltpu.make_async_copy(weight_hbm, weight, local_sem.at[3])
    get_weight.start()

    group = 2 * replicas
    line = owners // 4
    in_group = y * replicas + r

    def group_peer(o):
        other = lax.rem(in_group + o, group)
        return ((z * 2 + lax.div(other, replicas)) * 2 + core, lax.rem(other, replicas))

    def line_peer(o):
        return ((lax.rem(z + o, line) * 2 + y) * 2 + core, r)

    greeted = [(right, r), (left, r), (mate, r)]
    greeted += [(b, lax.rem(r + o, replicas)) for o in range(1, replicas)]
    if pieces:
        greeted += [group_peer(o) for o in range(1, group)] + [line_peer(o) for o in range(1, line)]
    barrier = pltpu.get_barrier_semaphore()
    for peer in greeted:
        pl.semaphore_signal(barrier, inc=1, device_id=peer, device_id_type=MESH)
    pl.semaphore_wait(barrier, len(greeted))

    sent = []

    def start(copy):
        copy.start()
        sent.append(copy)

    def send_own(s):
        for u in range(2):
            for d in range(2):
                start(ring(d, s, u, 0, b))
        for u in range(2):
            start(to_mate(0, s, u, 0, b))

    def arrive(s, h):
        for u in range(2):
            for d in range(2):
                if h > reach(d, u):
                    continue
                block = from_me(d, h)
                ring(d, s, u, h - 1, block).wait_recv()
                if h + 1 <= reach(d, u):
                    start(ring(d, s, u, h, block))
                start(to_mate(d, s, u, h, block))

    def arrive_mate(s, h):
        for u in range(2):
            for d in range(2):
                if h == 0:
                    if d == 0:
                        to_mate(0, s, u, 0, mate).wait_recv()
                elif h <= reach(d, u):
                    to_mate(d, s, u, h, mate_of(from_me(d, h))).wait_recv()

    tiles[slots] = jnp.zeros((tile, tile), BF16)
    count = count_ref[0, 0]

    def fill(source, first):
        picked = [jnp.int32(slots)] * (row_tiles * col_tiles)
        run = jnp.int32(0)
        for k in range(MOST):
            slot = first + k
            safe = jnp.minimum(slot, slots - 1)
            q = cols_ref[0, 0, safe]
            ok = (slot < count) & (q >= source * col_tiles) & (q < (source + 1) * col_tiles)
            key = jnp.where(ok, rows_ref[0, 0, safe] * col_tiles + q - source * col_tiles, -1)
            run = run + ok.astype(jnp.int32)
            picked = [jnp.where(key == at, slot, old) for at, old in enumerate(picked)]
        for at, slot in enumerate(picked):
            i, j = at // col_tiles, at % col_tiles
            dense[source, i * tile:(i + 1) * tile, j * tile:(j + 1) * tile] = tiles[slot]
        return first + run

    def product(s, part, block):
        a = dense[block, pl.ds(pl.multiple_of(part * here, here), here), :]
        return jnp.dot(a, gath[s, block], preferred_element_type=F32)

    def multiply(s, part, blocks):
        total = acc[s, part]
        for block in blocks:
            total = total + product(s, part, block)
        acc[s, part] = total

    many = replicas > 2

    def multiply_all(s, h):
        if many:
            def step(part, carry):
                multiply(s, part, blocks_at(h))
                return carry
            lax.fori_loop(0, replicas, step, 0)
        else:
            for part in range(replicas):
                multiply(s, part, blocks_at(h))

    def blocks_at(h):
        if h == 0:
            return [b, mate]
        ones = [from_me(0, h)] if h == far else [from_me(0, h), from_me(1, h)]
        return ones + [mate_of(block) for block in ones]

    def to_rep(s, o):
        return pltpu.make_async_remote_copy(
            src_ref=(xsend0, xsend1)[s].at[o - 1], dst_ref=(xrecv0, xrecv1)[s].at[o - 1],
            send_sem=x_send.at[s, o - 1], recv_sem=x_recv.at[s, o - 1],
            device_id=(b, lax.rem(r + o, replicas)), device_id_type=MESH,
        )

    def settle(s):
        total = acc[s, r]
        for o in range(1, replicas):
            to_rep(s, o).wait_recv()
            total = total + (xrecv0, xrecv1)[s][o - 1].astype(F32)
        agg[s] = total.astype(BF16)

    own[0].wait()
    own[1].wait()
    send_own(0)
    get_tiles.wait()
    first = jnp.int32(0)
    acc[...] = jnp.zeros(acc.shape, F32)
    first = lax.fori_loop(0, far, fill, first)
    for h in range(1, far + 1):
        arrive(0, h)
        if h == 1:
            send_own(1)
            lax.fori_loop(far, owners, fill, first)
            continue
        arrive(1, h - 1)
        for done in range(h - 2, h) if h == 2 else (h - 1,):
            arrive_mate(0, done)
            multiply_all(0, done)
        arrive_mate(1, h - 2)
        multiply_all(1, h - 2)
    arrive_mate(0, far)
    if many:
        multiply_all(0, far)
    for o in range(1, replicas):
        part = lax.rem(r + o, replicas)
        if not many:
            multiply(0, part, blocks_at(far))
        xsend0[o - 1] = acc[0, part]
        start(to_rep(0, o))
    arrive_mate(1, far - 1)
    multiply_all(1, far - 1)
    arrive(1, far)
    if not many:
        multiply(0, r, blocks_at(far))
    arrive_mate(1, far)
    if many:
        multiply_all(1, far)
    for o in range(1, replicas):
        part = lax.rem(r + o, replicas)
        if not many:
            multiply(1, part, blocks_at(far))
        xsend1[o - 1] = acc[1, part].astype(BF16)
        start(to_rep(1, o))
    if not many:
        multiply(1, r, blocks_at(far))
    settle(0)
    get_weight.wait()
    pre[...] = jnp.dot(agg[0], weight[0:half, :], preferred_element_type=F32) + bias_ref[...]
    settle(1)

    rows = 64
    for at in range(0, here, rows):
        p = pre[at:at + rows, :] + jnp.dot(agg[1, at:at + rows, :], weight[half:, :], preferred_element_type=F32)
        sig = 1.0 / (1.0 + jnp.exp(-p))
        hidden_ref[at:at + rows, :] = (p * sig).astype(BF16)
        slope[at:at + rows, :] = sig * (1.0 + p * (1.0 - sig))
    wide = hidden_ref[...].astype(F32)
    scores = lax.dot_general(
        head_ref[...], wide, (((1,), (1,)), ((), ())), precision=lax.Precision.HIGHEST, preferred_element_type=F32
    )
    scale_log = scores[0:1, :]
    raw = scores[1:2, :]
    shape_param = jnp.maximum(raw, 0.0) + jnp.log1p(jnp.exp(-jnp.abs(raw))) + 0.5
    log_ratio = jnp.log(times_ref[...]) - scale_log
    hazard = jnp.exp(shape_param * log_ratio)
    observed = events_ref[...].astype(F32)
    norm = 1.0 / math.sqrt(here * owners * replicas)
    grad_scale = (observed * shape_param - shape_param * hazard) * norm
    grad_shape = (
        (hazard * log_ratio - observed * (1.0 / shape_param + log_ratio)) * (1.0 / (1.0 + jnp.exp(-raw))) * norm
    )
    stacked = jnp.concatenate([grad_scale, grad_shape, jnp.zeros((6, here), F32)], axis=0)
    sm_send[0, 1:3, :] = jnp.dot(stacked, wide, precision=lax.Precision.HIGHEST, preferred_element_type=F32)[0:2]
    upright = stacked.T
    bias_sum = jnp.zeros((1, width), F32)
    for at in range(0, here, rows):
        gh = upright[at:at + rows, 0:1] * head_ref[0:1, :] + upright[at:at + rows, 1:2] * head_ref[1:2, :]
        gp = gh * slope[at:at + rows, :]
        bias_sum = bias_sum + jnp.sum(gp, axis=0, keepdims=True)
        pre[at:at + rows, :] = gp
    sm_send[0, 0:1, :] = bias_sum
    sm_send[0, 3:8, :] = jnp.zeros((5, width), F32)
    gp_bf = pre[...].astype(BF16)

    def grad_half(s):
        return lax.dot_general(agg[s], gp_bf, (((0,), (0,)), ((), ())), preferred_element_type=F32)

    if not pieces:
        gw_ref[0:half, :] = grad_half(0)
        gw_ref[half:, :] = grad_half(1)
        small_ref[...] = sm_send[0]
    else:
        big, mid, low = pieces

        def remote(src, dst, sems, at, peer):
            return pltpu.make_async_remote_copy(
                src_ref=src, dst_ref=dst, send_sem=sems[0].at[at], recv_sem=sems[1].at[at],
                device_id=peer, device_id_type=MESH,
            )

        gs, ss = (g_send, g_recv), (s_send, s_recv)
        partner = (mate, r)
        base = core * big

        def from_group(o):
            return lax.rem(in_group + group - o, group)

        def from_line(o):
            return lax.rem(z + line - o, line)

        def piece(start_row, member, count):
            return pl.ds(pl.multiple_of(start_row + member * count, count), count)

        c_small = remote(sm_send.at[0], sm1, ss, 0, partner)
        start(c_small)
        g1s[...] = grad_half(1 - core).astype(BF16)
        order = [lax.rem(in_group + o, group) for o in range(1, group)] + [in_group]
        copies1 = []
        for at, member in enumerate(order):
            rows_of = piece(0, member, mid)
            copies1.append(remote(g1s.at[rows_of], g1r.at[rows_of], gs, at, partner))
            start(copies1[-1])
        gsum[...] = grad_half(core)
        c_small.wait_recv()
        sm_send[1] = sm_send[0] + sm1[...]
        small2 = [remote(sm_send.at[1], sm2.at[o - 1], ss, o, group_peer(o)) for o in range(1, group)]
        for copy in small2:
            start(copy)
        used = group
        copies = []
        for o in range(1, group):
            rows_of = piece(0, order[o - 1], mid)
            copies1[o - 1].wait_recv()
            g2s[o - 1] = (gsum[rows_of, :] + g1r[rows_of, :].astype(F32)).astype(BF16)
            copies.append(remote(g2s.at[o - 1], g2r.at[o - 1], gs, used + o - 1, group_peer(o)))
            start(copies[-1])
        used += group - 1
        copies1[group - 1].wait_recv()
        first_row = in_group * mid
        rows_of = piece(0, in_group, mid)
        total = gsum[rows_of, :] + g1r[rows_of, :].astype(F32)
        for copy in small2:
            copy.wait_recv()
        small_total = sm_send[1]
        for o in range(1, group):
            small_total = small_total + sm2[o - 1]
        sm_send[2] = small_total
        small3 = [remote(sm_send.at[2], sm3.at[o - 1], ss, group - 1 + o, line_peer(o)) for o in range(1, line)]
        for copy in small3:
            start(copy)
        for o in range(1, group):
            copies[o - 1].wait_recv()
            total = total + g2r[o - 1].astype(F32)
        gsum[rows_of, :] = total
        copies = []
        for o in range(1, line):
            g3s[o - 1] = gsum[piece(first_row, lax.rem(z + o, line), low), :].astype(BF16)
            copies.append(remote(g3s.at[o - 1], g3r.at[o - 1], gs, used + o - 1, line_peer(o)))
            start(copies[-1])
        used += line - 1
        total = gsum[piece(first_row, z, low), :]
        for o in range(1, line):
            copies[o - 1].wait_recv()
            total = total + g3r[o - 1].astype(F32)
        gw_ref[piece(base + first_row, z, low), :] = total.astype(BF16)

        def along_line(o, member):
            ref = gw_ref.at[piece(base + first_row, member, low)]
            return remote(ref, ref, gs, used + o - 1, line_peer(o))

        def in_plane(o, lo, from_member):
            ref = gw_ref.at[piece(base + from_member * mid, from_line(lo), low)]
            return remote(ref, ref, gs, used + (line - 1) + (o - 1) * line + lo, group_peer(o))

        def over_chip(o, lo, half_base):
            ref = gw_ref.at[piece(half_base + from_group(o) * mid, from_line(lo), low)]
            return remote(ref, ref, gs, used + (line - 1) + (group - 1) * line + o * line + lo, partner)

        for o in range(1, line):
            start(along_line(o, z))
        for lo in range(line):
            if lo:
                along_line(lo, from_line(lo)).wait_recv()
            for o in range(1, group):
                start(in_plane(o, lo, in_group))
            start(over_chip(0, lo, base))
        for copy in small3:
            copy.wait_recv()
        small_total = sm_send[2]
        for o in range(1, line):
            small_total = small_total + sm3[o - 1]
        small_ref[...] = small_total
        for lo in range(line):
            for o in range(1, group):
                in_plane(o, lo, from_group(o)).wait_recv()
                start(over_chip(o, lo, base))
        for lo in range(line):
            for o in range(group):
                over_chip(o, lo, (1 - core) * big).wait_recv()
    for copy in sent:
        copy.wait_send()


def finish(hidden_in, gw_in, small_in, hidden_out, gw_out, bias_out, head_out):
    hidden_out[...] = hidden_in[...]
    gw_out[...] = gw_in[...].astype(F32)
    bias_out[...] = small_in[0, :]
    head_out[...] = small_in[1:3, :]


def local(owners, replicas, features, tile_values, tile_rows, tile_cols, tile_counts, weight, bias, head, times, events):
    here, width = features.shape
    half = width // 2
    slots, tile = tile_values.shape[2], tile_values.shape[3]
    pieces = fused_sum_rows(owners, replicas, width)
    far = owners // 4
    group, line = 2 * replicas, max(owners // 4, 2)
    big, mid, low = pieces or (16, 16, 16)
    vmem = pl.BlockSpec(memory_space=pltpu.VMEM)
    smem = pl.BlockSpec(memory_space=pltpu.SMEM)
    hbm = pl.BlockSpec(memory_space=pl.ANY)
    dma = pltpu.SemaphoreType.DMA
    g_count = 2 * group + 2 * line + 2 * group * line
    hidden, grad_weight, small = pl.pallas_call(
        functools.partial(kernel, owners, replicas, pieces),
        out_shape=(
            jax.ShapeDtypeStruct((here, width), BF16),
            jax.ShapeDtypeStruct((width, width), BF16 if pieces else F32),
            jax.ShapeDtypeStruct((8, width), F32),
        ),
        in_specs=[hbm, hbm, smem, smem, smem, hbm, vmem, vmem, vmem, vmem],
        out_specs=(vmem, vmem, vmem),
        scratch_shapes=[
            pltpu.VMEM((2, owners, here, half), BF16),
            pltpu.VMEM((owners, here * replicas, here), BF16),
            pltpu.VMEM((slots + 1, tile, tile), BF16),
            pltpu.VMEM((width, width), BF16),
            pltpu.VMEM((2, replicas, here, half), F32),
            pltpu.VMEM((replicas - 1, here, half), F32),
            pltpu.VMEM((replicas - 1, here, half), F32),
            pltpu.VMEM((replicas - 1, here, half), BF16),
            pltpu.VMEM((replicas - 1, here, half), BF16),
            pltpu.VMEM((2, here, half), BF16),
            pltpu.VMEM((here, width), F32),
            pltpu.VMEM((here, width), F32),
            pltpu.VMEM((big, width), F32),
            pltpu.VMEM((big, width), BF16),
            pltpu.VMEM((big, width), BF16),
            pltpu.VMEM((group - 1, mid, width), BF16),
            pltpu.VMEM((group - 1, mid, width), BF16),
            pltpu.VMEM((line - 1, low, width), BF16),
            pltpu.VMEM((line - 1, low, width), BF16),
            pltpu.VMEM((3, 8, width), F32),
            pltpu.VMEM((8, width), F32),
            pltpu.VMEM((group - 1, 8, width), F32),
            pltpu.VMEM((line - 1, 8, width), F32),
            dma((4,)),
            dma((2, 2, 2, far)),
            dma((2, 2, 2, far)),
            dma((2, 2, 2, far + 1)),
            dma((2, 2, 2, far + 1)),
            dma((2, replicas - 1)),
            dma((2, replicas - 1)),
            dma((g_count,)),
            dma((g_count,)),
            dma((group + line,)),
            dma((group + line,)),
        ],
        compiler_params=pltpu.CompilerParams(
            collective_id=0, has_side_effects=True, vmem_limit_bytes=60 * 1024 * 1024
        ),
    )(
        features,
        tile_values.reshape(slots, tile, tile),
        tile_rows,
        tile_cols,
        tile_counts,
        weight,
        bias.reshape(1, width),
        head,
        times.reshape(1, here),
        events.reshape(1, here),
    )
    if not pieces:
        grad_weight, small = lax.psum((grad_weight, small), ("blk", "rep"))
    return pl.pallas_call(
        finish,
        out_shape=(
            jax.ShapeDtypeStruct((here, width), BF16),
            jax.ShapeDtypeStruct((width, width), F32),
            jax.ShapeDtypeStruct((width,), F32),
            jax.ShapeDtypeStruct((2, width), F32),
        ),
        in_specs=[vmem, vmem, vmem],
        out_specs=(vmem, vmem, vmem, vmem),
    )(hidden, grad_weight, small)


def solution(mesh):
    placed = (
        P(("blk", "rep"), None),
        P("blk", "rep", None, None, None),
        P("blk", "rep", None),
        P("blk", "rep", None),
        P("blk", "rep"),
        P(),
        P(),
        P(),
        P(("blk", "rep")),
        P(("blk", "rep")),
    )
    return jax.shard_map(
        functools.partial(local, mesh.shape["blk"], mesh.shape["rep"]),
        mesh=mesh,
        in_specs=placed,
        out_specs=(P(("blk", "rep"), None), P(), P(), P()),
        check_vma=False,
    )
```
